768 devices in a mesh: rep: 48 (over z_lo, y), mp: 16 (over z_hi, x, core).
Axes of the slice: x: 4, y: 8, z: 12 (z_hi: 2, z_lo: 6; z = z_hi * 6 + z_lo), core: 2. Of those that a mesh axis runs over, the one named last changes fastest.
Arguments:
- local_weights: bfloat16 [48, 2, 192, 14336], P('rep', None, None, 'mp'), may hold values from -6 to 6
- base_weights: float32 [2, 192, 14336], P(None, None, 'mp'), may hold values from -6 to 6
- momentum: float32 [2, 192, 14336], P(None, 'rep', 'mp'), may hold values from -4 to 4
- exponents: int32 [48, 2, 192, 112], P('rep', None, None, 'mp'), may hold values from -10 to 0
- mix_ratio: int32 [2], replicated, may hold values from 1 to 16, as said below
Outputs:
- mixed_weights: bfloat16 [48, 2, 192, 14336], P('rep', None, None, 'mp')
- new_base: float32 [2, 192, 14336], P(None, None, 'mp')
- new_momentum: float32 [2, 192, 14336], P(None, 'rep', 'mp')
The draws below stay inside these ranges and needn't reach their ends.
Inputs may be any that keep to these rules, and one draw needn't show every extreme that they name: mix_ratio[1] is 16 and mix_ratio[0] lies in 1 to 15.
All inputs are finite; a program needn't handle non-finite values.
Results may differ from the reference program's by a relative error of at most 0.012.
Values may be sent and summed in bfloat16 or wider, within the bound.
No kernel may reach another device: no remote copies, remote signals or barrier semaphores. Data moves between devices by JAX's collectives and lax.ppermute only.
A program may use at most 32 MiB of HBM per device.

```python
import jax
import jax.numpy as jnp
from jax import lax

FF = 14336
BLOCK = 128
ROWS = 192
REPLICAS = 48
N_REP = 48


def draw_mix_ratio(key, part):
    key = jax.random.fold_in(key, 7)
    numerator = jax.random.randint(key, (), 1, 16)
    denominator = jnp.full((), 16, jnp.int32)
    return jnp.stack([numerator, denominator]).astype(jnp.int32)


def place_ends(result, stream_key, least, high):
    dims = result.shape
    index_at = [jax.random.randint(jax.random.fold_in(stream_key, axis), (), 0, dims[axis]) for axis in range(len(dims))]
    result = result.at[tuple(index_at)].set(least)
    longest = dims.index(max(dims))
    index_at[longest] = (index_at[longest] + 1) % dims[longest]
    return result.at[tuple(index_at)].set(high)


def shard_levels(own_key, dims, pieces, smallest, top_value):
    def one(dim, parts):
        steps = jax.random.uniform(jax.random.fold_in(jax.random.fold_in(own_key, 6), dim), (parts,), jnp.float32, smallest / len(pieces), top_value / len(pieces))
        return jnp.repeat(jnp.exp(steps), dims[dim] // parts).reshape((-1,) + (1,) * (len(dims) - dim - 1))

    level = one(*pieces[0])
    for cut in pieces[1:]:
        level = level * one(*cut)
    return level


def normal_values(rng, dims, spread, reach, cuts=(), kind=jnp.bfloat16):
    loudness = shard_levels(rng, dims, cuts, -0.22, 0.18) if cuts else 1.0
    values = jax.random.normal(rng, dims, jnp.float32) * spread * loudness
    return jnp.minimum(jnp.maximum(values, -reach), reach).astype(kind)


def setup_inputs(seed: int = 0) -> dict:
    key_list = jax.random.split(jax.random.key(seed), 6)
    local_weights = normal_values(key_list[0], (REPLICAS, 2, ROWS, FF), 1.0, 6.0, ((0, 48), (3, 16)))
    base_weights = normal_values(key_list[1], (2, ROWS, FF), 1.0, 6.0, ((2, 16),), jnp.float32)
    momentum = normal_values(key_list[2], (2, ROWS, FF), 0.5, 4.0, ((1, 48), (2, 16)), jnp.float32)
    exponents = place_ends(jax.random.randint(key_list[3], (REPLICAS, 2, ROWS, FF // BLOCK), -10, 1), jax.random.fold_in(key_list[3], 1), -10, 0).astype(jnp.int32)
    mix_ratio = draw_mix_ratio(jax.random.fold_in(key_list[5], 71), 0)
    return {"local_weights": local_weights, "base_weights": base_weights, "momentum": momentum, "exponents": exponents, "mix_ratio": mix_ratio}


def reference(local_weights, base_weights, momentum, exponents, mix_ratio):
    groups = FF // BLOCK

    def add_term(total, items):
        local_one, expo_one = items
        scales = jnp.exp2(expo_one.astype(jnp.float32))[..., None]
        delta = (base_weights - local_one.astype(jnp.float32)).reshape(2, ROWS, groups, BLOCK)
        coded = jnp.clip(delta / scales, -448.0, 448.0).astype(jnp.bfloat16)
        return total + (coded.astype(jnp.float32) * scales).reshape(2, ROWS, FF), None

    start = jnp.zeros((2, ROWS, FF), jnp.float32)
    total, unused = lax.scan(add_term, start, (local_weights, exponents))
    average = total / N_REP
    new_momentum = 0.9 * momentum + average
    new_base = base_weights - 0.7 * (average + 0.9 * new_momentum)
    alpha = mix_ratio[0].astype(jnp.float32) / mix_ratio[1].astype(jnp.float32)
    mixed_weights = (alpha * local_weights.astype(jnp.float32) + (1.0 - alpha) * new_base[None]).astype(jnp.bfloat16)
    return mixed_weights, new_base, new_momentum
```

```python
import functools

import jax
import jax.numpy as jnp
from jax import lax
from jax.experimental import pallas as pl
from jax.experimental.pallas import tpu as pltpu
from jax.sharding import PartitionSpec as P

BLOCK = 128
OUTER = 3
F32 = jnp.float32
BF16 = jnp.bfloat16


def low_rows(shape):
    return lax.broadcasted_iota(jnp.int32, shape, len(shape) - 2) < 4


def encode_kernel(groups, local_ref, base_ref, exp_ref, out_ref):
    width = base_ref.shape[3]
    pieces = [[], [], [], []]
    for outer in range(OUTER):
        halves = []
        for side in range(2):
            delta = base_ref[side, outer] - local_ref[side, outer].astype(F32)
            bound = exp_ref[side, outer]
            bound = jnp.concatenate(
                [jnp.broadcast_to(bound[:, g : g + 1], (16, BLOCK)) for g in range(groups)], axis=1
            )
            coded = jnp.minimum(jnp.maximum(delta, -bound), bound)
            halves.append(coded.reshape(2, 8, width))
        gate, up = halves
        low = low_rows(gate.shape)
        even = jnp.where(low, gate, pltpu.roll(up, 4, 1))
        odd = jnp.where(low, pltpu.roll(gate, 4, 1), up)
        for k in range(2):
            pieces[2 * k].append(even[k])
            pieces[2 * k + 1].append(odd[k])
    for i in range(4):
        out_ref[i] = jnp.concatenate(pieces[i], axis=0).astype(BF16)


def partial_kernel(parts, replicas, outer_ref, got_ref, momentum_ref, send_ref, own_ref):
    mine = outer_ref[0]
    total = got_ref[0].astype(F32)
    for i in range(1, parts):
        total = total + got_ref[i].astype(F32)
    total = total * (1.0 / replicas)
    share = 0.81 * momentum_ref[...]
    own = jnp.zeros_like(share)
    rows = []
    for outer in range(OUTER):
        average = total[8 * outer : 8 * outer + 8]
        here = mine == outer
        own = jnp.where(here, average, own)
        rows.append(1.9 * average + jnp.where(here, share, 0.0))
    own_ref[...] = own
    send = jnp.concatenate(rows, axis=0).astype(BF16)
    for i in range(OUTER):
        send_ref[i] = send


def step_kernel(parts, outer_ref, got_ref, momentum_ref, own_ref, send_ref, new_ref):
    mine = outer_ref[0]
    blocks = [got_ref[i].astype(F32) for i in range(OUTER)]
    total = blocks[0]
    for block in blocks[1:]:
        total = total + block
    send = (0.7 * total).astype(BF16)
    for i in range(parts):
        send_ref[i] = send
    others = jnp.zeros_like(own_ref[...])
    for i in range(OUTER):
        picked = jnp.zeros_like(others)
        for outer in range(OUTER):
            picked = jnp.where(mine == outer, blocks[i][8 * outer : 8 * outer + 8], picked)
        others = others + jnp.where(mine == i, 0.0, picked)
    average = own_ref[...] + others * (1.0 / 1.9)
    new_ref[...] = 0.9 * momentum_ref[...] + average


def mix_kernel(mix_ref, got_ref, local_ref, base_ref, mixed_ref, new_ref):
    width = base_ref.shape[3]
    top = jnp.full((16, width), mix_ref[0].astype(F32))
    bottom = jnp.full((16, width), mix_ref[1].astype(F32))
    alpha = top / bottom
    blocks = [got_ref[i].astype(F32) for i in range(4)]
    for outer in range(OUTER):
        rows = slice(8 * outer, 8 * outer + 8)
        even = jnp.stack([blocks[0][rows], blocks[2][rows]])
        odd = jnp.stack([blocks[1][rows], blocks[3][rows]])
        low = low_rows(even.shape)
        gate = jnp.where(low, even, pltpu.roll(odd, 4, 1)).reshape(16, width)
        up = jnp.where(low, pltpu.roll(even, 4, 1), odd).reshape(16, width)
        for side, update in ((0, gate), (1, up)):
            fresh = base_ref[side, outer] - update
            new_ref[side, outer] = fresh
            kept = local_ref[side, outer].astype(F32)
            mixed_ref[side, outer] = (alpha * kept + (1.0 - alpha) * fresh).astype(BF16)


def shards(local_weights, base_weights, momentum, exponents, mix_ratio):
    replicas = lax.axis_size("rep")
    rows = base_weights.shape[1]
    width = base_weights.shape[2]
    groups = exponents.shape[3]
    parts = replicas // OUTER
    steps = parts // 4
    deep = rows // OUTER
    near = [[o * parts + j for j in range(parts)] for o in range(OUTER)]
    far = [[o * parts + j for o in range(OUTER)] for j in range(parts)]
    outer = (lax.axis_index("rep") // parts).astype(jnp.int32).reshape(1)

    local = local_weights.reshape(2, OUTER, deep, width)
    base = base_weights.reshape(2, OUTER, deep, width)
    bound = (448.0 * jnp.exp2(exponents[0].astype(F32))).reshape(2, OUTER, deep, groups)
    tall = pl.BlockSpec((2, OUTER, 16, width), lambda i: (0, 0, i, 0))
    flat = pl.BlockSpec((4, OUTER * 8, width), lambda i: (i, 0, 0))
    coded = pl.pallas_call(
        functools.partial(encode_kernel, groups),
        grid=(steps,),
        in_specs=[tall, tall, pl.BlockSpec((2, OUTER, 16, groups), lambda i: (0, 0, i, 0))],
        out_specs=flat,
        out_shape=jax.ShapeDtypeStruct((parts, OUTER * 8, width), BF16),
        name="encode",
    )(local, base, bound)
    got = lax.all_to_all(coded, "rep", 0, 0, axis_index_groups=near, tiled=True)
    held = momentum.reshape(8, width)
    scalar = pl.BlockSpec(memory_space=pltpu.SMEM)
    whole = pl.BlockSpec(memory_space=pltpu.VMEM)
    send, own = pl.pallas_call(
        functools.partial(partial_kernel, parts, replicas),
        in_specs=[scalar, whole, whole],
        out_specs=[whole, whole],
        out_shape=[
            jax.ShapeDtypeStruct((OUTER, OUTER * 8, width), BF16),
            jax.ShapeDtypeStruct((8, width), F32),
        ],
        name="partial",
    )(outer, got, held)
    got = lax.all_to_all(send, "rep", 0, 0, axis_index_groups=far, tiled=True)
    send, new_momentum = pl.pallas_call(
        functools.partial(step_kernel, parts),
        in_specs=[scalar, whole, whole, whole],
        out_specs=[whole, whole],
        out_shape=[
            jax.ShapeDtypeStruct((parts, OUTER * 8, width), BF16),
            jax.ShapeDtypeStruct((8, width), F32),
        ],
        name="outer_step",
    )(outer, got, held, own)
    got = lax.all_to_all(send, "rep", 0, 0, axis_index_groups=near, tiled=True)
    mixed, new_base = pl.pallas_call(
        mix_kernel,
        grid=(steps,),
        in_specs=[scalar, flat, tall, tall],
        out_specs=[tall, tall],
        out_shape=[
            jax.ShapeDtypeStruct(local.shape, BF16),
            jax.ShapeDtypeStruct(base.shape, F32),
        ],
        name="mix",
    )(mix_ratio, got, local, base)
    return (
        mixed.reshape(local_weights.shape),
        new_base.reshape(base_weights.shape),
        new_momentum.reshape(momentum.shape),
    )


def solution(mesh):
    placed = (
        P("rep", None, None, "mp"),
        P(None, None, "mp"),
        P(None, "rep", "mp"),
        P("rep", None, None, "mp"),
        P(),
    )
    return jax.shard_map(
        shards,
        mesh=mesh,
        in_specs=placed,
        out_specs=(P("rep", None, None, "mp"), P(None, None, "mp"), P(None, "rep", "mp")),
        check_vma=False,
    )
```

```python
import functools

import jax
import jax.numpy as jnp
from jax import lax
from jax.experimental import pallas as pl
from jax.experimental.pallas import tpu as pltpu
from jax.sharding import PartitionSpec as P

BLOCK = 128
OUTER = 2
ROUND = 8
TALL = 16
F32 = jnp.float32
BF16 = jnp.bfloat16
SMALL = pltpu.CompilerParams(vmem_limit_bytes=12 << 20)
SCALAR = pl.BlockSpec(memory_space=pltpu.SMEM)
WHOLE = pl.BlockSpec(memory_space=pltpu.VMEM)
FAR = pl.BlockSpec(memory_space=pltpu.HBM)


def slot(member):
    layer = member // ROUND
    return (layer ^ 1 if layer < 2 else layer) * ROUND + member % ROUND


def low_rows(shape):
    return lax.broadcasted_iota(jnp.int32, shape, len(shape) - 2) < 4


def encode_kernel(place_ref, exp_hbm, local_hbm, base_hbm, out_ref, rows_ref, exp_ref, local_ref, base_ref, bound_ref, sems):
    _, _, deep, width = base_ref.shape
    steps = deep // TALL
    load_exp = pltpu.make_async_copy(exp_hbm, exp_ref, sems.at[2 * steps])
    load_exp.start()
    loads = []
    for step in range(steps):
        rows = pl.ds(TALL * step, TALL)
        for k, (source, target) in enumerate(((local_hbm, local_ref), (base_hbm, base_ref))):
            load = pltpu.make_async_copy(source.at[:, :, rows], target.at[:, :, rows], sems.at[2 * step + k])
            load.start()
            loads.append(load)
    load_exp.wait()
    groups = exp_ref.shape[0]
    where = lax.broadcasted_iota(jnp.int32, (groups, width), 1) // BLOCK
    spread = (where == lax.broadcasted_iota(jnp.int32, (groups, width), 0)).astype(BF16)
    for side in range(2):
        power = (1 << (exp_ref[:, side, :] + 10)).astype(F32) * (448.0 / 1024.0)
        bound_ref[side] = lax.dot_general(
            power.astype(BF16), spread, (((0,), (0,)), ((), ())), preferred_element_type=F32
        )
    tiles = TALL // 8
    for step in range(steps):
        rows = pl.ds(TALL * step, TALL)
        loads[2 * step].wait()
        loads[2 * step + 1].wait()
        pieces = [[] for _ in range(2 * tiles)]
        for outer in range(OUTER):
            halves = []
            for side in range(2):
                delta = base_ref[side, outer, rows] - local_ref[side, outer, rows].astype(F32)
                bound = bound_ref[side, pl.ds(outer * deep + TALL * step, TALL)]
                coded = jnp.minimum(jnp.maximum(delta, -bound), bound)
                halves.append(coded.reshape(tiles, 8, width))
            gate, up = halves
            low = low_rows(gate.shape)
            even = jnp.where(low, gate, pltpu.roll(up, 4, 1))
            odd = jnp.where(low, pltpu.roll(gate, 4, 1), up)
            for k in range(tiles):
                pieces[2 * k].append(even[k])
                pieces[2 * k + 1].append(odd[k])
        for i in range(2 * tiles):
            out_ref[slot(2 * tiles * step + i)] = jnp.concatenate(pieces[i], axis=0).astype(BF16)
    odd = place_ref[1] == 1
    mine = pl.ds(pl.multiple_of(place_ref[2] * 8, 8), 8)
    low = low_rows((8, width))
    for outer in range(OUTER):
        gate, up = base_ref[0, outer, mine], base_ref[1, outer, mine]
        first = jnp.where(odd, pltpu.roll(gate, 4, 0), gate)
        second = jnp.where(odd, up, pltpu.roll(up, 4, 0))
        rows_ref[8 * outer : 8 * outer + 8] = jnp.where(low, first, second)


def partial_kernel(parts, replicas, place_ref, got_ref, rows_ref, momentum_ref, send_ref, own_ref, share_ref):
    mine = place_ref[0]
    share_ref[0:4] = 0.567 * momentum_ref[0]
    share_ref[4:8] = 0.567 * momentum_ref[1]
    total = got_ref[0].astype(F32)
    for i in range(1, parts):
        total = total + got_ref[i].astype(F32)
    base = rows_ref[...]
    exact = base * (1.0 / OUTER) - total * (1.33 / replicas)
    share = share_ref[...]
    own = jnp.zeros_like(share)
    sums = []
    for outer in range(OUTER):
        rows = slice(8 * outer, 8 * outer + 8)
        here = mine == outer
        part = exact[rows] - jnp.where(here, share, 0.0)
        rounded = part.astype(BF16)
        own = jnp.where(here, base[rows] - share - (part - rounded.astype(F32)), own)
        sums.append(part)
    own_ref[...] = own
    send_ref[...] = jnp.concatenate(sums, axis=0).astype(BF16)


def step_kernel(parts, place_ref, kept_ref, got_ref, momentum_ref, own_ref, send_ref, new_ref):
    mine = place_ref[0]
    total = kept_ref[...].astype(F32) + got_ref[...].astype(F32)
    send = total.astype(BF16)
    for i in range(parts):
        send_ref[i] = send
    picked = total[0:8]
    for outer in range(1, OUTER):
        picked = jnp.where(mine == outer, total[8 * outer : 8 * outer + 8], picked)
    average = (own_ref[...] - picked) * (1.0 / 1.33)
    for side in range(2):
        new_ref[side] = 0.9 * momentum_ref[side] + average[4 * side : 4 * side + 4]


def mix_kernel(mix_ref, got_ref, local_ref, mixed_hbm, new_hbm, mixed_ref, new_ref, sems):
    _, _, deep, width = new_ref.shape
    tiles = TALL // 8
    top = jnp.full((8, width), mix_ref[0].astype(F32))
    bottom = jnp.full((8, width), mix_ref[1].astype(F32))
    alpha = (top / bottom)[None]
    stores = []
    for step in range(deep // TALL):
        span = pl.ds(TALL * step, TALL)
        blocks = [got_ref[slot(2 * tiles * step + i)].astype(F32) for i in range(2 * tiles)]
        for outer in range(OUTER):
            rows = slice(8 * outer, 8 * outer + 8)
            even = jnp.stack([blocks[2 * k][rows] for k in range(tiles)])
            odd = jnp.stack([blocks[2 * k + 1][rows] for k in range(tiles)])
            low = low_rows(even.shape)
            gate = jnp.where(low, even, pltpu.roll(odd, 4, 1))
            up = jnp.where(low, pltpu.roll(even, 4, 1), odd)
            for side, fresh in ((0, gate), (1, up)):
                new_ref[side, outer, span] = fresh.reshape(TALL, width)
                kept = local_ref[side, outer, span].astype(F32).reshape(tiles, 8, width)
                mixed = alpha * kept + (1.0 - alpha) * fresh
                mixed_ref[side, outer, span] = mixed.reshape(TALL, width).astype(BF16)
        for k, (source, target) in enumerate(((mixed_ref, mixed_hbm), (new_ref, new_hbm))):
            store = pltpu.make_async_copy(source.at[:, :, span], target.at[:, :, span], sems.at[2 * step + k])
            store.start()
            stores.append(store)
    for store in stores:
        store.wait()


def encode(place, exponents, local, base):
    groups, _, rows = exponents.shape
    _, _, deep, width = base.shape
    return pl.pallas_call(
        encode_kernel,
        in_specs=[SCALAR, FAR, FAR, FAR],
        out_specs=[WHOLE, WHOLE],
        out_shape=[
            jax.ShapeDtypeStruct((deep // 4, OUTER * 8, width), BF16),
            jax.ShapeDtypeStruct((OUTER * 8, width), F32),
        ],
        scratch_shapes=[
            pltpu.VMEM(exponents.shape, jnp.int32),
            pltpu.VMEM(local.shape, BF16),
            pltpu.VMEM(base.shape, F32),
            pltpu.VMEM((2, rows, width), F32),
            pltpu.SemaphoreType.DMA((2 * (deep // TALL) + 1,)),
        ],
        compiler_params=SMALL,
        name="encode",
    )(place, *(pltpu.with_memory_space_constraint(x, pltpu.HBM) for x in (exponents, local, base)))


def partial(replicas, place, got, rows, momentum):
    parts, tall, width = got.shape
    return pl.pallas_call(
        functools.partial(partial_kernel, parts, replicas),
        in_specs=[SCALAR, WHOLE, WHOLE, WHOLE],
        out_specs=[WHOLE, WHOLE],
        out_shape=[jax.ShapeDtypeStruct((tall, width), BF16), jax.ShapeDtypeStruct((8, width), F32)],
        scratch_shapes=[pltpu.VMEM((8, width), F32)],
        compiler_params=SMALL,
        name="partial",
    )(place, got, rows, momentum)


def outer_step(parts, place, kept, got, momentum, own):
    tall, width = got.shape
    return pl.pallas_call(
        functools.partial(step_kernel, parts),
        in_specs=[SCALAR, WHOLE, WHOLE, WHOLE, WHOLE],
        out_specs=[WHOLE, WHOLE],
        out_shape=[jax.ShapeDtypeStruct((parts, tall, width), BF16), jax.ShapeDtypeStruct(momentum.shape, F32)],
        compiler_params=SMALL,
        name="outer_step",
    )(place, kept, got, momentum, own)


def mix(mix_ratio, got, local):
    deep = local.shape[2]
    return pl.pallas_call(
        mix_kernel,
        in_specs=[SCALAR, WHOLE, WHOLE],
        out_specs=[FAR, FAR],
        out_shape=[jax.ShapeDtypeStruct(local.shape, BF16), jax.ShapeDtypeStruct(local.shape, F32)],
        scratch_shapes=[
            pltpu.VMEM(local.shape, BF16),
            pltpu.VMEM(local.shape, F32),
            pltpu.SemaphoreType.DMA((2 * (deep // TALL),)),
        ],
        compiler_params=SMALL,
        name="mix",
    )(mix_ratio, got, local)


def shards(local_weights, base_weights, momentum, exponents, mix_ratio):
    replicas = lax.axis_size("rep")
    rows, width = base_weights.shape[1:]
    parts = replicas // OUTER
    members = sorted(range(parts), key=slot)
    near = [[o * parts + j for j in members] for o in range(OUTER)]
    across = [(r, (r + parts) % replicas) for r in range(replicas)]
    index = lax.axis_index("rep")
    member = lax.rem(index, parts)
    place = jnp.stack([lax.div(index, parts), lax.rem(member, 2), lax.div(member, 2)]).astype(jnp.int32)
    swap = functools.partial(
        lax.all_to_all, axis_name="rep", split_axis=0, concat_axis=0, axis_index_groups=near, tiled=True
    )

    local = local_weights.reshape(2, OUTER, rows // OUTER, width)
    base = base_weights.reshape(2, OUTER, rows // OUTER, width)
    coded, own_rows = encode(place, jnp.transpose(exponents[0], (2, 0, 1)), local, base)
    sent, own = partial(replicas, place, swap(coded), own_rows, momentum)
    got = lax.ppermute(sent, "rep", across)
    sent, new_momentum = outer_step(parts, place, sent, got, momentum, own)
    mixed, new_base = mix(mix_ratio, swap(sent), local)
    return mixed.reshape(local_weights.shape), new_base.reshape(base_weights.shape), new_momentum


def solution(mesh):
    placed = (
        P("rep", None, None, "mp"),
        P(None, None, "mp"),
        P(None, "rep", "mp"),
        P("rep", None, None, "mp"),
        P(),
    )
    return jax.shard_map(
        shards,
        mesh=mesh,
        in_specs=placed,
        out_specs=(P("rep", None, None, "mp"), P(None, None, "mp"), P(None, "rep", "mp")),
        check_vma=False,
    )
```

```python
import functools

import jax
import jax.numpy as jnp
from jax import lax
from jax.experimental import pallas as pl
from jax.experimental.pallas import tpu as pltpu
from jax.sharding import PartitionSpec as P

BLOCK = 128
OUTER = 2
ROUND = 8
TALL = 16
F32 = jnp.float32
BF16 = jnp.bfloat16
SMALL = pltpu.CompilerParams(vmem_limit_bytes=12 << 20)
SCALAR = pl.BlockSpec(memory_space=pltpu.SMEM)
WHOLE = pl.BlockSpec(memory_space=pltpu.VMEM)
FAR = pl.BlockSpec(memory_space=pltpu.HBM)


FIRST_IN = (1, 4)
FIRST_OUT = (1, 0)


def slot(member, first):
    layer, y = member // ROUND - first[0], member % ROUND - first[1]
    return layer % 3 * ROUND + y % ROUND


def low_rows(shape):
    return lax.broadcasted_iota(jnp.int32, shape, len(shape) - 2) < 4


def encode_kernel(place_ref, exp_hbm, local_hbm, base_hbm, out_ref, rows_ref, exp_ref, local_ref, base_ref, bound_ref, sems):
    _, _, deep, width = base_ref.shape
    steps = deep // TALL
    load_exp = pltpu.make_async_copy(exp_hbm, exp_ref, sems.at[2 * steps])
    load_exp.start()
    loads = []
    for step in range(steps):
        rows = pl.ds(TALL * step, TALL)
        for k, (source, target) in enumerate(((local_hbm, local_ref), (base_hbm, base_ref))):
            load = pltpu.make_async_copy(source.at[:, :, rows], target.at[:, :, rows], sems.at[2 * step + k])
            load.start()
            loads.append(load)
    load_exp.wait()
    groups = exp_ref.shape[0]
    where = lax.broadcasted_iota(jnp.int32, (groups, width), 1) // BLOCK
    spread = (where == lax.broadcasted_iota(jnp.int32, (groups, width), 0)).astype(BF16)
    for side in range(2):
        power = (1 << (exp_ref[:, side, :] + 10)).astype(F32) * (448.0 / 1024.0)
        bound_ref[side] = lax.dot_general(
            power.astype(BF16), spread, (((0,), (0,)), ((), ())), preferred_element_type=F32
        )
    tiles = TALL // 8
    for step in range(steps):
        rows = pl.ds(TALL * step, TALL)
        loads[2 * step].wait()
        loads[2 * step + 1].wait()
        pieces = [[] for _ in range(2 * tiles)]
        for outer in range(OUTER):
            halves = []
            for side in range(2):
                delta = base_ref[side, outer, rows] - local_ref[side, outer, rows].astype(F32)
                bound = bound_ref[side, pl.ds(outer * deep + TALL * step, TALL)]
                coded = jnp.minimum(jnp.maximum(delta, -bound), bound)
                halves.append(coded.reshape(tiles, 8, width))
            gate, up = halves
            low = low_rows(gate.shape)
            even = jnp.where(low, gate, pltpu.roll(up, 4, 1))
            odd = jnp.where(low, pltpu.roll(gate, 4, 1), up)
            for k in range(tiles):
                pieces[2 * k].append(even[k])
                pieces[2 * k + 1].append(odd[k])
        for i in range(2 * tiles):
            out_ref[slot(2 * tiles * step + i, FIRST_IN)] = jnp.concatenate(pieces[i], axis=0).astype(BF16)
    odd = place_ref[1] == 1
    mine = pl.ds(pl.multiple_of(place_ref[2] * 8, 8), 8)
    low = low_rows((8, width))
    for outer in range(OUTER):
        gate, up = base_ref[0, outer, mine], base_ref[1, outer, mine]
        first = jnp.where(odd, pltpu.roll(gate, 4, 0), gate)
        second = jnp.where(odd, up, pltpu.roll(up, 4, 0))
        rows_ref[8 * outer : 8 * outer + 8] = jnp.where(low, first, second)


def partial_kernel(parts, replicas, place_ref, got_ref, rows_ref, momentum_ref, send_ref, own_ref, share_ref):
    mine = place_ref[0]
    share_ref[0:4] = 0.567 * momentum_ref[0]
    share_ref[4:8] = 0.567 * momentum_ref[1]
    total = got_ref[0].astype(F32)
    for i in range(1, parts):
        total = total + got_ref[i].astype(F32)
    base = rows_ref[...]
    exact = base * (1.0 / OUTER) - total * (1.33 / replicas)
    share = share_ref[...]
    own = jnp.zeros_like(share)
    sums = []
    for outer in range(OUTER):
        rows = slice(8 * outer, 8 * outer + 8)
        here = mine == outer
        part = exact[rows] - jnp.where(here, share, 0.0)
        rounded = part.astype(BF16)
        own = jnp.where(here, base[rows] - share - (part - rounded.astype(F32)), own)
        sums.append(part)
    own_ref[...] = own
    send_ref[...] = jnp.concatenate(sums, axis=0).astype(BF16)


def step_kernel(place_ref, kept_ref, got_ref, own_ref, send_ref, average_ref):
    mine = place_ref[0]
    total = kept_ref[...].astype(F32) + got_ref[...].astype(F32)
    send = total.astype(BF16)
    for i in range(send_ref.shape[0]):
        send_ref[i] = send
    picked = total[0:8]
    for outer in range(1, OUTER):
        picked = jnp.where(mine == outer, total[8 * outer : 8 * outer + 8], picked)
    average_ref[...] = (own_ref[...] - picked) * (1.0 / 1.33)


def mix_kernel(
    mix_ref, got_ref, local_ref, momentum_ref, average_ref,
    mixed_hbm, new_hbm, next_hbm, mixed_ref, new_ref, next_ref, sems,
):
    _, _, deep, width = new_ref.shape
    tiles = TALL // 8
    top = jnp.full((8, width), mix_ref[0].astype(F32))
    bottom = jnp.full((8, width), mix_ref[1].astype(F32))
    alpha = (top / bottom)[None]
    for side in range(2):
        next_ref[side] = 0.9 * momentum_ref[side] + average_ref[4 * side : 4 * side + 4]
    stores = [pltpu.make_async_copy(next_ref, next_hbm, sems.at[2 * (deep // TALL)])]
    stores[0].start()
    for step in range(deep // TALL):
        span = pl.ds(TALL * step, TALL)
        blocks = [got_ref[slot(2 * tiles * step + i, FIRST_OUT)].astype(F32) for i in range(2 * tiles)]
        for outer in range(OUTER):
            rows = slice(8 * outer, 8 * outer + 8)
            even = jnp.stack([blocks[2 * k][rows] for k in range(tiles)])
            odd = jnp.stack([blocks[2 * k + 1][rows] for k in range(tiles)])
            low = low_rows(even.shape)
            gate = jnp.where(low, even, pltpu.roll(odd, 4, 1))
            up = jnp.where(low, pltpu.roll(even, 4, 1), odd)
            for side, fresh in ((0, gate), (1, up)):
                new_ref[side, outer, span] = fresh.reshape(TALL, width)
                kept = local_ref[side, outer, span].astype(F32).reshape(tiles, 8, width)
                mixed = alpha * kept + (1.0 - alpha) * fresh
                mixed_ref[side, outer, span] = mixed.reshape(TALL, width).astype(BF16)
        for k, (source, target) in enumerate(((mixed_ref, mixed_hbm), (new_ref, new_hbm))):
            store = pltpu.make_async_copy(source.at[:, :, span], target.at[:, :, span], sems.at[2 * step + k])
            store.start()
            stores.append(store)
    for store in stores:
        store.wait()


def encode(place, exponents, local, base):
    groups, _, rows = exponents.shape
    _, _, deep, width = base.shape
    return pl.pallas_call(
        encode_kernel,
        in_specs=[SCALAR, FAR, FAR, FAR],
        out_specs=[WHOLE, WHOLE],
        out_shape=[
            jax.ShapeDtypeStruct((deep // 4, OUTER * 8, width), BF16),
            jax.ShapeDtypeStruct((OUTER * 8, width), F32),
        ],
        scratch_shapes=[
            pltpu.VMEM(exponents.shape, jnp.int32),
            pltpu.VMEM(local.shape, BF16),
            pltpu.VMEM(base.shape, F32),
            pltpu.VMEM((2, rows, width), F32),
            pltpu.SemaphoreType.DMA((2 * (deep // TALL) + 1,)),
        ],
        compiler_params=SMALL,
        name="encode",
    )(place, *(pltpu.with_memory_space_constraint(x, pltpu.HBM) for x in (exponents, local, base)))


def partial(replicas, place, got, rows, momentum):
    parts, tall, width = got.shape
    return pl.pallas_call(
        functools.partial(partial_kernel, parts, replicas),
        in_specs=[SCALAR, WHOLE, WHOLE, WHOLE],
        out_specs=[WHOLE, WHOLE],
        out_shape=[jax.ShapeDtypeStruct((tall, width), BF16), jax.ShapeDtypeStruct((8, width), F32)],
        scratch_shapes=[pltpu.VMEM((8, width), F32)],
        compiler_params=SMALL,
        name="partial",
    )(place, got, rows, momentum)


def outer_step(parts, place, kept, got, own):
    tall, width = got.shape
    return pl.pallas_call(
        step_kernel,
        in_specs=[SCALAR, WHOLE, WHOLE, WHOLE],
        out_specs=[WHOLE, WHOLE],
        out_shape=[jax.ShapeDtypeStruct((parts, tall, width), BF16), jax.ShapeDtypeStruct(own.shape, F32)],
        compiler_params=SMALL,
        name="outer_step",
    )(place, kept, got, own)


def mix(mix_ratio, got, local, momentum, average):
    deep = local.shape[2]
    return pl.pallas_call(
        mix_kernel,
        in_specs=[SCALAR, WHOLE, WHOLE, WHOLE, WHOLE],
        out_specs=[FAR, FAR, FAR],
        out_shape=[
            jax.ShapeDtypeStruct(local.shape, BF16),
            jax.ShapeDtypeStruct(local.shape, F32),
            jax.ShapeDtypeStruct(momentum.shape, F32),
        ],
        scratch_shapes=[
            pltpu.VMEM(local.shape, BF16),
            pltpu.VMEM(local.shape, F32),
            pltpu.VMEM(momentum.shape, F32),
            pltpu.SemaphoreType.DMA((2 * (deep // TALL) + 1,)),
        ],
        compiler_params=SMALL,
        name="mix",
    )(mix_ratio, got, local, momentum, average)


def shards(local_weights, base_weights, momentum, exponents, mix_ratio):
    replicas = lax.axis_size("rep")
    rows, width = base_weights.shape[1:]
    parts = replicas // OUTER
    near_in, near_out = (
        [[o * parts + j for j in sorted(range(parts), key=lambda j: slot(j, first))] for o in range(OUTER)]
        for first in (FIRST_IN, FIRST_OUT)
    )
    across = [(r, (r + parts) % replicas) for r in range(replicas)]
    index = lax.axis_index("rep")
    member = lax.rem(index, parts)
    place = jnp.stack([lax.div(index, parts), lax.rem(member, 2), lax.div(member, 2)]).astype(jnp.int32)
    swap = functools.partial(lax.all_to_all, axis_name="rep", split_axis=0, concat_axis=0, tiled=True)

    local = local_weights.reshape(2, OUTER, rows // OUTER, width)
    base = base_weights.reshape(2, OUTER, rows // OUTER, width)
    coded, own_rows = encode(place, jnp.transpose(exponents[0], (2, 0, 1)), local, base)
    sent, own = partial(replicas, place, swap(coded, axis_index_groups=near_in), own_rows, momentum)
    got = lax.ppermute(sent, "rep", across)
    sent, average = outer_step(parts, place, sent, got, own)
    mixed, new_base, new_momentum = mix(mix_ratio, swap(sent, axis_index_groups=near_out), local, momentum, average)
    return mixed.reshape(local_weights.shape), new_base.reshape(base_weights.shape), new_momentum


def solution(mesh):
    placed = (
        P("rep", None, None, "mp"),
        P(None, None, "mp"),
        P(None, "rep", "mp"),
        P("rep", None, None, "mp"),
        P(),
    )
    return jax.shard_map(
        shards,
        mesh=mesh,
        in_specs=placed,
        out_specs=(P("rep", None, None, "mp"), P(None, None, "mp"), P(None, "rep", "mp")),
        check_vma=False,
    )
```

```python
import functools

import jax
import jax.numpy as jnp
from jax import lax
from jax.experimental import pallas as pl
from jax.experimental.pallas import tpu as pltpu
from jax.sharding import PartitionSpec as P

BLOCK = 128
OUTER = 2
ROUND = 8
TALL = 32
F32 = jnp.float32
BF16 = jnp.bfloat16
SMALL = pltpu.CompilerParams(vmem_limit_bytes=12 << 20)
SCALAR = pl.BlockSpec(memory_space=pltpu.SMEM)
WHOLE = pl.BlockSpec(memory_space=pltpu.VMEM)
FAR = pl.BlockSpec(memory_space=pltpu.HBM)


FIRST_IN = (1, 4)
FIRST_OUT = (2, 0)


def slot(member, first):
    layer, y = member // ROUND - first[0], member % ROUND - first[1]
    return layer % 3 * ROUND + y % ROUND


def low_rows(shape):
    return lax.broadcasted_iota(jnp.int32, shape, len(shape) - 2) < 4


def encode_kernel(place_ref, exp_hbm, local_hbm, base_hbm, out_ref, rows_ref, exp_ref, local_ref, base_ref, bound_ref, sems):
    _, _, deep, width = base_ref.shape
    steps = deep // TALL
    load_exp = pltpu.make_async_copy(exp_hbm, exp_ref, sems.at[2 * steps])
    load_exp.start()
    loads = []
    for step in range(steps):
        rows = pl.ds(TALL * step, TALL)
        for k, (source, target) in enumerate(((local_hbm, local_ref), (base_hbm, base_ref))):
            load = pltpu.make_async_copy(source.at[:, :, rows], target.at[:, :, rows], sems.at[2 * step + k])
            load.start()
            loads.append(load)
    load_exp.wait()
    groups = exp_ref.shape[0]
    where = lax.broadcasted_iota(jnp.int32, (groups, width), 1) // BLOCK
    spread = (where == lax.broadcasted_iota(jnp.int32, (groups, width), 0)).astype(BF16)
    for side in range(2):
        power = (1 << (exp_ref[:, side, :] + 10)).astype(F32) * (448.0 / 1024.0)
        bound_ref[side] = lax.dot_general(
            power.astype(BF16), spread, (((0,), (0,)), ((), ())), preferred_element_type=F32
        )
    tiles = TALL // 8
    for step in range(steps):
        rows = pl.ds(TALL * step, TALL)
        loads[2 * step].wait()
        loads[2 * step + 1].wait()
        pieces = [[] for _ in range(2 * tiles)]
        for outer in range(OUTER):
            halves = []
            for side in range(2):
                delta = base_ref[side, outer, rows] - local_ref[side, outer, rows].astype(F32)
                bound = bound_ref[side, pl.ds(outer * deep + TALL * step, TALL)]
                coded = jnp.minimum(jnp.maximum(delta, -bound), bound)
                halves.append(coded.reshape(tiles, 8, width))
            gate, up = halves
            low = low_rows(gate.shape)
            even = jnp.where(low, gate, pltpu.roll(up, 4, 1))
            odd = jnp.where(low, pltpu.roll(gate, 4, 1), up)
            for k in range(tiles):
                pieces[2 * k].append(even[k])
                pieces[2 * k + 1].append(odd[k])
        for i in range(2 * tiles):
            out_ref[slot(2 * tiles * step + i, FIRST_IN)] = jnp.concatenate(pieces[i], axis=0).astype(BF16)
    odd = place_ref[1] == 1
    mine = pl.ds(pl.multiple_of(place_ref[2] * 8, 8), 8)
    low = low_rows((8, width))
    for outer in range(OUTER):
        gate, up = base_ref[0, outer, mine], base_ref[1, outer, mine]
        first = jnp.where(odd, pltpu.roll(gate, 4, 0), gate)
        second = jnp.where(odd, up, pltpu.roll(up, 4, 0))
        rows_ref[8 * outer : 8 * outer + 8] = jnp.where(low, first, second)


def partial_kernel(parts, replicas, place_ref, got_ref, rows_ref, momentum_ref, send_ref, own_ref, share_ref):
    mine = place_ref[0]
    share_ref[0:4] = 0.567 * momentum_ref[0]
    share_ref[4:8] = 0.567 * momentum_ref[1]
    total = got_ref[0].astype(F32)
    for i in range(1, parts):
        total = total + got_ref[i].astype(F32)
    base = rows_ref[...]
    exact = base * (1.0 / OUTER) - total * (1.33 / replicas)
    share = share_ref[...]
    own = jnp.zeros_like(share)
    sums = []
    for outer in range(OUTER):
        rows = slice(8 * outer, 8 * outer + 8)
        here = mine == outer
        part = exact[rows] - jnp.where(here, share, 0.0)
        rounded = part.astype(BF16)
        own = jnp.where(here, base[rows] - share - (part - rounded.astype(F32)), own)
        sums.append(part)
    own_ref[...] = own
    send_ref[...] = jnp.concatenate(sums, axis=0).astype(BF16)


def step_kernel(place_ref, kept_ref, got_ref, own_ref, send_ref, average_ref):
    mine = place_ref[0]
    total = kept_ref[...].astype(F32) + got_ref[...].astype(F32)
    send = total.astype(BF16)
    for i in range(send_ref.shape[0]):
        send_ref[i] = send
    picked = total[0:8]
    for outer in range(1, OUTER):
        picked = jnp.where(mine == outer, total[8 * outer : 8 * outer + 8], picked)
    average_ref[...] = (own_ref[...] - picked) * (1.0 / 1.33)


def mix_kernel(
    mix_ref, got_ref, local_ref, momentum_ref, average_ref,
    mixed_hbm, new_hbm, next_hbm, mixed_ref, new_ref, next_ref, sems,
):
    _, _, deep, width = new_ref.shape
    tiles = TALL // 8
    top = jnp.full((8, width), mix_ref[0].astype(F32))
    bottom = jnp.full((8, width), mix_ref[1].astype(F32))
    alpha = (top / bottom)[None]
    for side in range(2):
        next_ref[side] = 0.9 * momentum_ref[side] + average_ref[4 * side : 4 * side + 4]
    stores = [pltpu.make_async_copy(next_ref, next_hbm, sems.at[2 * (deep // TALL)])]
    stores[0].start()
    for step in range(deep // TALL):
        span = pl.ds(TALL * step, TALL)
        blocks = [got_ref[slot(2 * tiles * step + i, FIRST_OUT)].astype(F32) for i in range(2 * tiles)]
        for outer in range(OUTER):
            rows = slice(8 * outer, 8 * outer + 8)
            even = jnp.stack([blocks[2 * k][rows] for k in range(tiles)])
            odd = jnp.stack([blocks[2 * k + 1][rows] for k in range(tiles)])
            low = low_rows(even.shape)
            gate = jnp.where(low, even, pltpu.roll(odd, 4, 1))
            up = jnp.where(low, pltpu.roll(even, 4, 1), odd)
            for side, fresh in ((0, gate), (1, up)):
                new_ref[side, outer, span] = fresh.reshape(TALL, width)
                kept = local_ref[side, outer, span].astype(F32).reshape(tiles, 8, width)
                mixed = alpha * kept + (1.0 - alpha) * fresh
                mixed_ref[side, outer, span] = mixed.reshape(TALL, width).astype(BF16)
        for k, (source, target) in enumerate(((mixed_ref, mixed_hbm), (new_ref, new_hbm))):
            store = pltpu.make_async_copy(source.at[:, :, span], target.at[:, :, span], sems.at[2 * step + k])
            store.start()
            stores.append(store)
    for store in stores:
        store.wait()


def encode(place, exponents, local, base):
    groups, _, rows = exponents.shape
    _, _, deep, width = base.shape
    return pl.pallas_call(
        encode_kernel,
        in_specs=[SCALAR, FAR, FAR, FAR],
        out_specs=[WHOLE, WHOLE],
        out_shape=[
            jax.ShapeDtypeStruct((deep // 4, OUTER * 8, width), BF16),
            jax.ShapeDtypeStruct((OUTER * 8, width), F32),
        ],
        scratch_shapes=[
            pltpu.VMEM(exponents.shape, jnp.int32),
            pltpu.VMEM(local.shape, BF16),
            pltpu.VMEM(base.shape, F32),
            pltpu.VMEM((2, rows, width), F32),
            pltpu.SemaphoreType.DMA((2 * (deep // TALL) + 1,)),
        ],
        compiler_params=SMALL,
        name="encode",
    )(place, *(pltpu.with_memory_space_constraint(x, pltpu.HBM) for x in (exponents, local, base)))


def partial(replicas, place, got, rows, momentum):
    parts, tall, width = got.shape
    return pl.pallas_call(
        functools.partial(partial_kernel, parts, replicas),
        in_specs=[SCALAR, WHOLE, WHOLE, WHOLE],
        out_specs=[WHOLE, WHOLE],
        out_shape=[jax.ShapeDtypeStruct((tall, width), BF16), jax.ShapeDtypeStruct((8, width), F32)],
        scratch_shapes=[pltpu.VMEM((8, width), F32)],
        compiler_params=SMALL,
        name="partial",
    )(place, got, rows, momentum)


def outer_step(parts, place, kept, got, own):
    tall, width = got.shape
    return pl.pallas_call(
        step_kernel,
        in_specs=[SCALAR, WHOLE, WHOLE, WHOLE],
        out_specs=[WHOLE, WHOLE],
        out_shape=[jax.ShapeDtypeStruct((parts, tall, width), BF16), jax.ShapeDtypeStruct(own.shape, F32)],
        compiler_params=SMALL,
        name="outer_step",
    )(place, kept, got, own)


def mix(mix_ratio, got, local, momentum, average):
    deep = local.shape[2]
    return pl.pallas_call(
        mix_kernel,
        in_specs=[SCALAR, WHOLE, WHOLE, WHOLE, WHOLE],
        out_specs=[FAR, FAR, FAR],
        out_shape=[
            jax.ShapeDtypeStruct(local.shape, BF16),
            jax.ShapeDtypeStruct(local.shape, F32),
            jax.ShapeDtypeStruct(momentum.shape, F32),
        ],
        scratch_shapes=[
            pltpu.VMEM(local.shape, BF16),
            pltpu.VMEM(local.shape, F32),
            pltpu.VMEM(momentum.shape, F32),
            pltpu.SemaphoreType.DMA((2 * (deep // TALL) + 1,)),
        ],
        compiler_params=SMALL,
        name="mix",
    )(mix_ratio, got, local, momentum, average)


def shards(local_weights, base_weights, momentum, exponents, mix_ratio):
    replicas = lax.axis_size("rep")
    rows, width = base_weights.shape[1:]
    parts = replicas // OUTER
    near_in, near_out = (
        [[o * parts + j for j in sorted(range(parts), key=lambda j: slot(j, first))] for o in range(OUTER)]
        for first in (FIRST_IN, FIRST_OUT)
    )
    across = [(r, (r + parts) % replicas) for r in range(replicas)]
    index = lax.axis_index("rep")
    member = lax.rem(index, parts)
    place = jnp.stack([lax.div(index, parts), lax.rem(member, 2), lax.div(member, 2)]).astype(jnp.int32)
    swap = functools.partial(lax.all_to_all, axis_name="rep", split_axis=0, concat_axis=0, tiled=True)

    local = local_weights.reshape(2, OUTER, rows // OUTER, width)
    base = base_weights.reshape(2, OUTER, rows // OUTER, width)
    coded, own_rows = encode(place, jnp.transpose(exponents[0], (2, 0, 1)), local, base)
    sent, own = partial(replicas, place, swap(coded, axis_index_groups=near_in), own_rows, momentum)
    got = lax.ppermute(sent, "rep", across)
    sent, average = outer_step(parts, place, sent, got, own)
    mixed, new_base, new_momentum = mix(mix_ratio, swap(sent, axis_index_groups=near_out), local, momentum, average)
    return mixed.reshape(local_weights.shape), new_base.reshape(base_weights.shape), new_momentum


def solution(mesh):
    placed = (
        P("rep", None, None, "mp"),
        P(None, None, "mp"),
        P(None, "rep", "mp"),
        P("rep", None, None, "mp"),
        P(),
    )
    return jax.shard_map(
        shards,
        mesh=mesh,
        in_specs=placed,
        out_specs=(P("rep", None, None, "mp"), P(None, None, "mp"), P(None, "rep", "mp")),
        check_vma=False,
    )
```

```python
import functools

import jax
import jax.numpy as jnp
from jax import lax
from jax.experimental import pallas as pl
from jax.experimental.pallas import tpu as pltpu
from jax.sharding import PartitionSpec as P

BLOCK = 128
OUTER = 2
ROUND = 8
TALL = 16
F32 = jnp.float32
BF16 = jnp.bfloat16
SMALL = pltpu.CompilerParams(vmem_limit_bytes=12 << 20)
SCALAR = pl.BlockSpec(memory_space=pltpu.SMEM)
WHOLE = pl.BlockSpec(memory_space=pltpu.VMEM)
FAR = pl.BlockSpec(memory_space=pltpu.HBM)


FIRST_IN = (2, 4)
FIRST_OUT = (0, 0)


def slot(member, first):
    layer, y = member // ROUND - first[0], member % ROUND - first[1]
    return layer % 3 * ROUND + y % ROUND


def low_rows(shape):
    return lax.broadcasted_iota(jnp.int32, shape, len(shape) - 2) < 4


def encode_kernel(place_ref, exp_hbm, local_hbm, base_hbm, out_ref, rows_ref, exp_ref, local_ref, base_ref, bound_ref, sems):
    _, _, deep, width = base_ref.shape
    steps = deep // TALL
    load_exp = pltpu.make_async_copy(exp_hbm, exp_ref, sems.at[2 * steps])
    load_exp.start()
    loads = []
    for step in range(steps):
        rows = pl.ds(TALL * step, TALL)
        for k, (source, target) in enumerate(((local_hbm, local_ref), (base_hbm, base_ref))):
            load = pltpu.make_async_copy(source.at[:, :, rows], target.at[:, :, rows], sems.at[2 * step + k])
            load.start()
            loads.append(load)
    load_exp.wait()
    groups = exp_ref.shape[0]
    where = lax.broadcasted_iota(jnp.int32, (groups, width), 1) // BLOCK
    spread = (where == lax.broadcasted_iota(jnp.int32, (groups, width), 0)).astype(BF16)
    for side in range(2):
        power = (1 << (exp_ref[:, side, :] + 10)).astype(F32) * (448.0 / 1024.0)
        bound_ref[side] = lax.dot_general(
            power.astype(BF16), spread, (((0,), (0,)), ((), ())), preferred_element_type=F32
        )
    tiles = TALL // 8
    for step in range(steps):
        rows = pl.ds(TALL * step, TALL)
        loads[2 * step].wait()
        loads[2 * step + 1].wait()
        pieces = [[] for _ in range(2 * tiles)]
        for outer in range(OUTER):
            halves = []
            for side in range(2):
                delta = base_ref[side, outer, rows] - local_ref[side, outer, rows].astype(F32)
                bound = bound_ref[side, pl.ds(outer * deep + TALL * step, TALL)]
                coded = jnp.minimum(jnp.maximum(delta, -bound), bound)
                halves.append(coded.reshape(tiles, 8, width))
            gate, up = halves
            low = low_rows(gate.shape)
            even = jnp.where(low, gate, pltpu.roll(up, 4, 1))
            odd = jnp.where(low, pltpu.roll(gate, 4, 1), up)
            for k in range(tiles):
                pieces[2 * k].append(even[k])
                pieces[2 * k + 1].append(odd[k])
        for i in range(2 * tiles):
            out_ref[slot(2 * tiles * step + i, FIRST_IN)] = jnp.concatenate(pieces[i], axis=0).astype(BF16)
    odd = place_ref[1] == 1
    mine = pl.ds(pl.multiple_of(place_ref[2] * 8, 8), 8)
    low = low_rows((8, width))
    for outer in range(OUTER):
        gate, up = base_ref[0, outer, mine], base_ref[1, outer, mine]
        first = jnp.where(odd, pltpu.roll(gate, 4, 0), gate)
        second = jnp.where(odd, up, pltpu.roll(up, 4, 0))
        rows_ref[8 * outer : 8 * outer + 8] = jnp.where(low, first, second)


def partial_kernel(parts, replicas, place_ref, got_ref, rows_ref, momentum_ref, send_ref, own_ref, share_ref):
    mine = place_ref[0]
    share_ref[0:4] = 0.567 * momentum_ref[0]
    share_ref[4:8] = 0.567 * momentum_ref[1]
    total = got_ref[0].astype(F32)
    for i in range(1, parts):
        total = total + got_ref[i].astype(F32)
    base = rows_ref[...]
    exact = base * (1.0 / OUTER) - total * (1.33 / replicas)
    share = share_ref[...]
    own = jnp.zeros_like(share)
    sums = []
    for outer in range(OUTER):
        rows = slice(8 * outer, 8 * outer + 8)
        here = mine == outer
        part = exact[rows] - jnp.where(here, share, 0.0)
        rounded = part.astype(BF16)
        own = jnp.where(here, base[rows] - share - (part - rounded.astype(F32)), own)
        sums.append(part)
    own_ref[...] = own
    send_ref[...] = jnp.concatenate(sums, axis=0).astype(BF16)


def step_kernel(place_ref, kept_ref, got_ref, own_ref, send_ref, average_ref):
    mine = place_ref[0]
    total = kept_ref[...].astype(F32) + got_ref[...].astype(F32)
    send = total.astype(BF16)
    for i in range(send_ref.shape[0]):
        send_ref[i] = send
    picked = total[0:8]
    for outer in range(1, OUTER):
        picked = jnp.where(mine == outer, total[8 * outer : 8 * outer + 8], picked)
    average_ref[...] = (own_ref[...] - picked) * (1.0 / 1.33)


def mix_kernel(
    mix_ref, got_ref, local_ref, momentum_ref, average_ref,
    mixed_hbm, new_hbm, next_hbm, mixed_ref, new_ref, next_ref, sems,
):
    _, _, deep, width = new_ref.shape
    tiles = TALL // 8
    top = jnp.full((8, width), mix_ref[0].astype(F32))
    bottom = jnp.full((8, width), mix_ref[1].astype(F32))
    alpha = (top / bottom)[None]
    for side in range(2):
        next_ref[side] = 0.9 * momentum_ref[side] + average_ref[4 * side : 4 * side + 4]
    stores = [pltpu.make_async_copy(next_ref, next_hbm, sems.at[2 * (deep // TALL)])]
    stores[0].start()
    for step in range(deep // TALL):
        span = pl.ds(TALL * step, TALL)
        blocks = [got_ref[slot(2 * tiles * step + i, FIRST_OUT)].astype(F32) for i in range(2 * tiles)]
        for outer in range(OUTER):
            rows = slice(8 * outer, 8 * outer + 8)
            even = jnp.stack([blocks[2 * k][rows] for k in range(tiles)])
            odd = jnp.stack([blocks[2 * k + 1][rows] for k in range(tiles)])
            low = low_rows(even.shape)
            gate = jnp.where(low, even, pltpu.roll(odd, 4, 1))
            up = jnp.where(low, pltpu.roll(even, 4, 1), odd)
            for side, fresh in ((0, gate), (1, up)):
                new_ref[side, outer, span] = fresh.reshape(TALL, width)
                kept = local_ref[side, outer, span].astype(F32).reshape(tiles, 8, width)
                mixed = alpha * kept + (1.0 - alpha) * fresh
                mixed_ref[side, outer, span] = mixed.reshape(TALL, width).astype(BF16)
        for k, (source, target) in enumerate(((mixed_ref, mixed_hbm), (new_ref, new_hbm))):
            store = pltpu.make_async_copy(source.at[:, :, span], target.at[:, :, span], sems.at[2 * step + k])
            store.start()
            stores.append(store)
    for store in stores:
        store.wait()


def encode(place, exponents, local, base):
    groups, _, rows = exponents.shape
    _, _, deep, width = base.shape
    return pl.pallas_call(
        encode_kernel,
        in_specs=[SCALAR, FAR, FAR, FAR],
        out_specs=[WHOLE, WHOLE],
        out_shape=[
            jax.ShapeDtypeStruct((deep // 4, OUTER * 8, width), BF16),
            jax.ShapeDtypeStruct((OUTER * 8, width), F32),
        ],
        scratch_shapes=[
            pltpu.VMEM(exponents.shape, jnp.int32),
            pltpu.VMEM(local.shape, BF16),
            pltpu.VMEM(base.shape, F32),
            pltpu.VMEM((2, rows, width), F32),
            pltpu.SemaphoreType.DMA((2 * (deep // TALL) + 1,)),
        ],
        compiler_params=SMALL,
        name="encode",
    )(place, *(pltpu.with_memory_space_constraint(x, pltpu.HBM) for x in (exponents, local, base)))


def partial(replicas, place, got, rows, momentum):
    parts, tall, width = got.shape
    return pl.pallas_call(
        functools.partial(partial_kernel, parts, replicas),
        in_specs=[SCALAR, WHOLE, WHOLE, WHOLE],
        out_specs=[WHOLE, WHOLE],
        out_shape=[jax.ShapeDtypeStruct((tall, width), BF16), jax.ShapeDtypeStruct((8, width), F32)],
        scratch_shapes=[pltpu.VMEM((8, width), F32)],
        compiler_params=SMALL,
        name="partial",
    )(place, got, rows, momentum)


def outer_step(parts, place, kept, got, own):
    tall, width = got.shape
    return pl.pallas_call(
        step_kernel,
        in_specs=[SCALAR, WHOLE, WHOLE, WHOLE],
        out_specs=[WHOLE, WHOLE],
        out_shape=[jax.ShapeDtypeStruct((parts, tall, width), BF16), jax.ShapeDtypeStruct(own.shape, F32)],
        compiler_params=SMALL,
        name="outer_step",
    )(place, kept, got, own)


def mix(mix_ratio, got, local, momentum, average):
    deep = local.shape[2]
    return pl.pallas_call(
        mix_kernel,
        in_specs=[SCALAR, WHOLE, WHOLE, WHOLE, WHOLE],
        out_specs=[FAR, FAR, FAR],
        out_shape=[
            jax.ShapeDtypeStruct(local.shape, BF16),
            jax.ShapeDtypeStruct(local.shape, F32),
            jax.ShapeDtypeStruct(momentum.shape, F32),
        ],
        scratch_shapes=[
            pltpu.VMEM(local.shape, BF16),
            pltpu.VMEM(local.shape, F32),
            pltpu.VMEM(momentum.shape, F32),
            pltpu.SemaphoreType.DMA((2 * (deep // TALL) + 1,)),
        ],
        compiler_params=SMALL,
        name="mix",
    )(mix_ratio, got, local, momentum, average)


def shards(local_weights, base_weights, momentum, exponents, mix_ratio):
    replicas = lax.axis_size("rep")
    rows, width = base_weights.shape[1:]
    parts = replicas // OUTER
    near_in, near_out = (
        [[o * parts + j for j in sorted(range(parts), key=lambda j: slot(j, first))] for o in range(OUTER)]
        for first in (FIRST_IN, FIRST_OUT)
    )
    across = [(r, (r + parts) % replicas) for r in range(replicas)]
    index = lax.axis_index("rep")
    member = lax.rem(index, parts)
    place = jnp.stack([lax.div(index, parts), lax.rem(member, 2), lax.div(member, 2)]).astype(jnp.int32)
    swap = functools.partial(lax.all_to_all, axis_name="rep", split_axis=0, concat_axis=0, tiled=True)

    local = local_weights.reshape(2, OUTER, rows // OUTER, width)
    base = base_weights.reshape(2, OUTER, rows // OUTER, width)
    coded, own_rows = encode(place, jnp.transpose(exponents[0], (2, 0, 1)), local, base)
    sent, own = partial(replicas, place, swap(coded, axis_index_groups=near_in), own_rows, momentum)
    got = lax.ppermute(sent, "rep", across)
    sent, average = outer_step(parts, place, sent, got, own)
    mixed, new_base, new_momentum = mix(mix_ratio, swap(sent, axis_index_groups=near_out), local, momentum, average)
    return mixed.reshape(local_weights.shape), new_base.reshape(base_weights.shape), new_momentum


def solution(mesh):
    placed = (
        P("rep", None, None, "mp"),
        P(None, None, "mp"),
        P(None, "rep", "mp"),
        P("rep", None, None, "mp"),
        P(),
    )
    return jax.shard_map(
        shards,
        mesh=mesh,
        in_specs=placed,
        out_specs=(P("rep", None, None, "mp"), P(None, None, "mp"), P(None, "rep", "mp")),
        check_vma=False,
    )
```
